1024 devices in a mesh: dp: 16 (over x, z_lo), shard: 64 (over z_hi, y, core).
Axes of the slice: x: 4, y: 8, z: 16 (z_hi: 4, z_lo: 4; z = z_hi * 4 + z_lo), core: 2. Of those that a mesh axis runs over, the one named last changes fastest.
Arguments:
- features: bfloat16 [2048, 4096], P('dp'), may hold values from -40 to 40
- out_grads: bfloat16 [2048, 16384], P('dp', 'shard'), may hold values from -120 to 120
- token_counts: int32 [16], replicated, may hold values from 42 to 128, as said below
- owner_order: int32 [32, 8], replicated, may hold values from 0 to 7, each once within a row
- moment: float32 [16384, 4096], P('shard', 'dp'), may hold values from -40 to 40
- second: float32 [16384, 4096], P('shard', 'dp'), may hold values from 0.03 to 1
- left_stat: float32 [64, 16, 128, 512], P('shard', 'dp'), may hold values from -0.5 to 2.5, as said below
- right_stat: float32 [64, 16, 128, 512], P('shard', 'dp'), may hold values from -0.5 to 2.5, as said below
- left_root: float32 [64, 16, 128, 512], P('shard', 'dp'), may hold values from -0.5 to 2, as said below
- right_root: float32 [64, 16, 128, 512], P('shard', 'dp'), may hold values from -0.5 to 2, as said below
Outputs:
- update: float32 [16384, 4096], P('shard', 'dp')
- new_moment: float32 [16384, 4096], P('shard', 'dp')
- new_second: float32 [16384, 4096], P('shard', 'dp')
- next_left: float32 [64, 16, 128, 512], P('shard', 'dp')
- next_right: float32 [64, 16, 128, 512], P('shard', 'dp')
The draws below stay inside these ranges and needn't reach their ends.
Inputs may be any that keep to these rules, and one draw needn't show every extreme that they name: The first token_counts[g] tokens of group g are live, the others padding. `owner_order`: each row is a permutation of 0 to 7. `left_stat`: each block's matrix is symmetric. `right_stat`: each block's matrix is symmetric. `left_root`: each block's matrix is symmetric. `right_root`: each block's matrix is symmetric.
All inputs are finite; a program needn't handle non-finite values.
Results may differ from the reference program's by a relative error of at most 0.00035.
Values may be sent and summed in bfloat16 or wider, within the bound.
No kernel may reach another device: no remote copies, remote signals or barrier semaphores. Data moves between devices by JAX's collectives and lax.ppermute only.
A program may use at most 32 MiB of HBM per device.

```python
import math
import jax
import jax.numpy as jnp
from jax import lax

BLOCK = 512
TOK_DEV = 128
QUARTER = 128
D = 4096
F = 16384
TOKENS = 2048
GROUPS = 16
BROWS = 32
QB = 8


def rough_scale(key, length, rise_factor):
    position = jnp.arange(length, dtype=jnp.float32) / length
    spread = jax.random.uniform(key, (length,), jnp.float32, 0.0, math.log(10.0))
    return jnp.exp(math.log(rise_factor) * position + spread)


def rough_values(key, rows, columns):
    subkeys = jax.random.split(key, 1)
    return jnp.clip(jax.random.normal(subkeys[0], (rows, columns), jnp.float32), -4.0, 4.0)


def to_left_drawn(matrix):
    shaped = matrix.reshape(BROWS, QB, 2, 2, QUARTER, BLOCK)
    return shaped.transpose(0, 2, 1, 3, 4, 5).reshape(2 * BROWS, 2 * QB, QUARTER, BLOCK)


def to_right_drawn(matrix):
    shaped = matrix.reshape(BROWS, QB, 2, 2, QUARTER, BLOCK)
    return shaped.transpose(0, 3, 1, 2, 4, 5).reshape(2 * BROWS, 2 * QB, QUARTER, BLOCK)


def symmetric(key, lower, upper, spread):
    subkeys = jax.random.split(key, 2)
    raw_normal = jnp.clip(jax.random.normal(subkeys[0], (BROWS, QB, BLOCK, BLOCK), jnp.float32), -4.0, 4.0)
    mixed = (raw_normal + jnp.swapaxes(raw_normal, 2, 3)) * (spread / math.sqrt(2.0 * BLOCK))
    diagonal = jax.random.uniform(subkeys[1], (BROWS, QB, BLOCK), jnp.float32, lower, upper)
    return mixed + diagonal[..., None] * jnp.eye(BLOCK, dtype=jnp.float32)


def draw_features(key, part):
    key = jax.random.fold_in(key, 1)
    subkeys = jax.random.split(key, 2)
    col_scale = rough_scale(subkeys[0], D, 3.0) / 3.0
    values = rough_values(subkeys[1], TOKENS, D)
    return (values * col_scale[None, :]).astype(jnp.bfloat16)


def draw_out_grads(key, part):
    key = jax.random.fold_in(key, 2)
    subkeys = jax.random.split(key, 2)
    col_scale = rough_scale(subkeys[0], F, 3.0)
    values = rough_values(subkeys[1], TOKENS, F)
    return (values * col_scale[None, :]).astype(jnp.bfloat16)


def draw_token_counts(key, part):
    key = jax.random.fold_in(key, 3)
    group_ids = jnp.arange(GROUPS, dtype=jnp.int32)
    base_count = TOK_DEV // 3 + 2 * TOK_DEV // 3 * group_ids // GROUPS
    jitter = jax.random.randint(key, (GROUPS,), 0, TOK_DEV // 6 + 1)
    values = jnp.minimum(base_count + jitter, TOK_DEV)
    return jnp.where(group_ids == GROUPS - 1, TOK_DEV, values).astype(jnp.int32)


def draw_moment(key, part):
    key = jax.random.fold_in(key, 4)
    subkeys = jax.random.split(key, 3)
    row_scale = rough_scale(subkeys[0], F, 3.0)
    col_scale = rough_scale(subkeys[1], D, 1.0)
    values = rough_values(subkeys[2], F, D)
    return values * row_scale[:, None] * col_scale[None, :] / 30.0


def draw_left_stat(key, part):
    key = jax.random.fold_in(key, 5)
    return to_left_drawn(symmetric(key, 0.5, 2.0, 0.5))


def draw_right_stat(key, part):
    key = jax.random.fold_in(key, 6)
    return to_right_drawn(symmetric(key, 0.5, 2.0, 0.5))


def draw_left_root(key, part):
    key = jax.random.fold_in(key, 7)
    return to_left_drawn(symmetric(key, 0.5, 1.5, 0.4))


def draw_right_root(key, part):
    key = jax.random.fold_in(key, 8)
    return to_right_drawn(symmetric(key, 0.5, 1.5, 0.4))


def levels(key, extent, pieces, least, top_value):
    factor_of, own = 1.0, jax.random.fold_in(key, 6)
    for dim, shards_of in pieces:
        heights = jnp.exp(jax.random.uniform(jax.random.fold_in(own, dim), (shards_of,), jnp.float32, least / len(pieces), top_value / len(pieces)))
        factor_of = factor_of * jnp.repeat(heights, extent[dim] // shards_of).reshape([-1 if axis == dim else 1 for axis in range(len(extent))])
    return factor_of


def setup_inputs(seed: int = 0) -> dict:
    arg_keys = jax.random.split(jax.random.key(seed), 11)
    return {
        "features": draw_features(jax.random.fold_in(arg_keys[10], 71), 0),
        "out_grads": draw_out_grads(jax.random.fold_in(arg_keys[10], 71), 0),
        "token_counts": draw_token_counts(jax.random.fold_in(arg_keys[10], 71), 0),
        "owner_order": jax.vmap(lambda own: jax.random.permutation(own, QB))(jax.random.split(arg_keys[3], BROWS)).reshape((BROWS, QB)).astype(jnp.int32),
        "moment": draw_moment(jax.random.fold_in(arg_keys[10], 71), 0),
        "second": jnp.clip(jnp.exp(math.log(1.0) - 3.506558 * jax.random.uniform(arg_keys[5], (F, D), jnp.float32) ** levels(arg_keys[5], (F, D), ((0, 64), (1, 16)), -0.2, 0.2)), 0.03, 1.0),
        "left_stat": draw_left_stat(jax.random.fold_in(arg_keys[10], 71), 0),
        "right_stat": draw_right_stat(jax.random.fold_in(arg_keys[10], 71), 0),
        "left_root": draw_left_root(jax.random.fold_in(arg_keys[10], 71), 0),
        "right_root": draw_right_root(jax.random.fold_in(arg_keys[10], 71), 0),
    }


def from_left(stored):
    shaped = stored.reshape(BROWS, 2, QB, 2, QUARTER, BLOCK)
    return shaped.transpose(0, 2, 1, 3, 4, 5).reshape(BROWS, QB, BLOCK, BLOCK)

def to_left(matrix):
    shaped = matrix.reshape(BROWS, QB, 2, 2, QUARTER, BLOCK)
    return shaped.transpose(0, 2, 1, 3, 4, 5).reshape(2 * BROWS, 2 * QB, QUARTER, BLOCK)

def from_right(stored):
    shaped = stored.reshape(BROWS, 2, QB, 2, QUARTER, BLOCK)
    return shaped.transpose(0, 2, 3, 1, 4, 5).reshape(BROWS, QB, BLOCK, BLOCK)

def to_right(matrix):
    shaped = matrix.reshape(BROWS, QB, 2, 2, QUARTER, BLOCK)
    return shaped.transpose(0, 3, 1, 2, 4, 5).reshape(2 * BROWS, 2 * QB, QUARTER, BLOCK)

def reference(features, out_grads, token_counts, owner_order, moment, second, left_stat, right_stat, left_root, right_root):
    position = jnp.arange(TOKENS, dtype=jnp.int32)
    group_id = position // TOK_DEV
    live_rows = position - group_id * TOK_DEV < token_counts[group_id]
    masked = jnp.where(live_rows[:, None], out_grads, jnp.zeros_like(out_grads))
    token_total = jnp.sum(token_counts).astype(jnp.float32)
    gradient = jnp.dot(masked.T, features, preferred_element_type=jnp.float32) / token_total
    grad_tiles = gradient.reshape(BROWS, BLOCK, QB, BLOCK)
    placed = jnp.take_along_axis(grad_tiles, owner_order[:, None, :, None].astype(jnp.int32), axis=2)
    owner_grad = placed.reshape(F, D)
    new_moment = 0.9 * moment + 0.1 * owner_grad
    new_second = 0.95 * second + 0.05 * owner_grad * owner_grad
    direction = new_moment / (jnp.sqrt(new_second) + 1e-08)
    blocks = placed.transpose(0, 2, 1, 3)
    exact = lax.Precision.HIGHEST
    left_gram = jnp.einsum('jkab,jkcb->jkac', blocks, blocks, precision=exact) / BLOCK
    right_gram = jnp.einsum('jkba,jkbc->jkac', blocks, blocks, precision=exact) / BLOCK
    next_left = to_left(0.95 * from_left(left_stat) + 0.05 * left_gram)
    next_right = to_right(0.95 * from_right(right_stat) + 0.05 * right_gram)
    inner_left = jnp.einsum('jkab,jkbc->jkac', from_left(left_root), blocks, precision=exact)
    precond = jnp.einsum('jkab,jkcb->jkac', inner_left, from_right(right_root), precision=exact)
    precond_flat = precond.transpose(0, 2, 1, 3).reshape(F, D)
    graft_scale = jnp.sqrt(jnp.sum(direction * direction) / (jnp.sum(precond_flat * precond_flat) + 1e-06))
    return (graft_scale * precond_flat, new_moment, new_second, next_left, next_right)
```

```python
import jax
import jax.numpy as jnp
from jax import lax
from jax.sharding import Mesh, PartitionSpec as P

DP = ("x", "zl")
SHARD = ("zh", "y", "c")
SIZES = (4, 4, 4, 8, 2)


def partner(value, axis, bit=0):
    return lax.ppermute(value, axis, [(i, i ^ 1 << bit) for i in range(lax.axis_size(axis))])


def stacked_rows(own_part, other_part, own_first):
    return jnp.where(
        own_first,
        jnp.concatenate([own_part, other_part], 0),
        jnp.concatenate([other_part, own_part], 0),
    )


def total_over_devices(values):
    tile = jnp.concatenate([jnp.full((4, 128), v, jnp.float32) for v in values], 0)
    tile = tile + partner(tile, "c")
    for axes in (("x", "y"), ("zh", "zl")):
        copies = jnp.broadcast_to(tile, (lax.axis_size(axes), *tile.shape))
        tile = jnp.sum(lax.all_to_all(copies, axes, split_axis=0, concat_axis=0, tiled=True), 0)
    return tile[0, 0], tile[4, 0]


def body(
    features,
    out_grads,
    token_counts,
    owner_order,
    moment,
    second,
    left_stat,
    right_stat,
    left_root,
    right_root,
):
    tok_rows = features.shape[0]
    half_rows = tok_rows // 2
    block_size = left_stat.shape[-1]
    half_size = block_size // 2
    quarter = block_size // 4
    block_count = features.shape[1] // block_size
    row_index = lax.axis_index(DP)
    side_bit = lax.axis_index("c")
    part_bit = lax.axis_index("zl") % 2
    precise = lax.Precision.HIGH
    token_total = jnp.sum(token_counts).astype(jnp.float32)
    block_perm = owner_order[lax.axis_index(("zh", "y"))]
    left_mine = left_root[0, 0]
    right_mine = right_root[0, 0]

    live_rows = jnp.arange(tok_rows) < token_counts[row_index]
    masked = jnp.where(live_rows[:, None], out_grads, jnp.zeros_like(out_grads))
    kept = lax.dynamic_slice_in_dim(masked, side_bit * half_rows, half_rows, 0)
    given = lax.dynamic_slice_in_dim(masked, (1 - side_bit) * half_rows, half_rows, 0)
    taken = partner(given, "c")
    own_first = side_bit == 0
    grads_half = jnp.where(
        own_first,
        jnp.concatenate([kept, taken], 1),
        jnp.concatenate([taken, kept], 1),
    )
    feats_half = lax.dynamic_slice_in_dim(features, side_bit * half_rows, half_rows, 0)
    blocks = [
        lax.dynamic_slice_in_dim(feats_half, block_perm[k] * block_size, block_size, 1)
        for k in range(block_count)
    ]
    outgoing = jnp.stack(
        [jnp.concatenate([blocks[k // 2], grads_half], 1) for k in range(2 * block_count)], 0
    )
    arrived = lax.all_to_all(outgoing, DP, split_axis=0, concat_axis=0, tiled=True)
    arrived = arrived.reshape(-1, 2 * block_size)
    partial = jnp.dot(
        arrived[:, block_size:].T, arrived[:, :block_size], preferred_element_type=jnp.float32
    )
    other_left = partner(left_mine, "zl")
    other_right = partner(right_mine, "c")
    whole_block = (partial + partner(partial, "c")) / token_total

    left_rows_root = stacked_rows(left_mine, other_left, part_bit == 0)
    right_rows_root = stacked_rows(right_mine, other_right, own_first)
    own_half = lax.dynamic_slice_in_dim(whole_block, side_bit * half_size, half_size, 0)
    left_rows = lax.dynamic_slice_in_dim(own_half, part_bit * quarter, quarter, 0)
    right_cols = lax.dynamic_slice_in_dim(
        whole_block, part_bit * half_size + side_bit * quarter, quarter, 1
    )
    tile_grad = lax.dynamic_slice_in_dim(own_half, part_bit * half_size, half_size, 1)
    new_moment = 0.9 * moment + 0.1 * tile_grad
    new_second = 0.95 * second + 0.05 * tile_grad * tile_grad
    direction = new_moment / (jnp.sqrt(new_second) + 1e-08)
    inner_left = jnp.dot(left_rows_root, whole_block, precision=precise)
    precond = jnp.dot(inner_left, right_rows_root.T, precision=precise)
    graft_totals = total_over_devices(
        (jnp.sum(direction * direction), jnp.sum(precond * precond))
    )
    next_left = 0.95 * left_stat[0, 0] + 0.05 * (
        jnp.dot(left_rows, whole_block.T, precision=precise) / block_size
    )
    next_right = 0.95 * right_stat[0, 0] + 0.05 * (
        jnp.dot(right_cols.T, whole_block, precision=precise) / block_size
    )
    graft_scale = jnp.sqrt(graft_totals[0] / (graft_totals[1] + 1e-06))
    return (
        graft_scale * precond,
        new_moment,
        new_second,
        next_left[None, None],
        next_right[None, None],
    )


def solution(mesh):
    fine = Mesh(mesh.devices.reshape(SIZES), DP + SHARD)
    return jax.shard_map(
        body,
        mesh=fine,
        in_specs=(
            P(DP, None),
            P(DP, SHARD),
            P(),
            P(),
            P(SHARD, DP),
            P(SHARD, DP),
            P(SHARD, DP, None, None),
            P(SHARD, DP, None, None),
            P(SHARD, DP, None, None),
            P(SHARD, DP, None, None),
        ),
        out_specs=(
            P(SHARD, DP),
            P(SHARD, DP),
            P(SHARD, DP),
            P(SHARD, DP, None, None),
            P(SHARD, DP, None, None),
        ),
        check_vma=False,
    )
```

```python
import jax
import jax.numpy as jnp
from jax import lax
from jax.experimental import pallas as pl
from jax.experimental.pallas import tpu as pltpu
from jax.sharding import Mesh, PartitionSpec as P

DP = ("x", "zl")
SHARD = ("zh", "y", "c")
SIZES = (4, 4, 4, 8, 2)
VMEM_LIMIT = 40 * 1024 * 1024


def partner(value, axis):
    return lax.ppermute(value, axis, [(i, i ^ 1) for i in range(lax.axis_size(axis))])


def split(value):
    high = value.astype(jnp.bfloat16)
    return high, (value - high.astype(jnp.float32)).astype(jnp.bfloat16)


def dot_rows(a, b):
    dims = (((1,), (1,)), ((), ()))
    mul = lambda p, q: lax.dot_general(p, q, dims, preferred_element_type=jnp.float32)
    return mul(a[0], b[0]) + (mul(a[0], b[1]) + mul(a[1], b[0]))


def dot_plain(a, b):
    dims = (((1,), (0,)), ((), ()))
    mul = lambda p, q: lax.dot_general(p, q, dims, preferred_element_type=jnp.float32)
    return mul(a[0], b[0]) + (mul(a[0], b[1]) + mul(a[1], b[0]))


def pack_kernel(counts_ref, order_ref, feats_ref, grads_ref, out_ref):
    half = feats_ref.shape[0] // 2
    fourth = half // 2
    width = out_ref.shape[2]
    side = lax.axis_index("c")
    group = lax.axis_index("x") * lax.axis_size("zl") + lax.axis_index("zl")
    brow = lax.axis_index("zh") * lax.axis_size("y") + lax.axis_index("y")
    count = counts_ref[group]
    rows = lax.broadcasted_iota(jnp.int32, grads_ref.shape, 0)
    masked = jnp.where(rows < count, grads_ref[...].astype(jnp.float32), 0.0)
    masked = masked.astype(jnp.bfloat16)
    for dest in range(out_ref.shape[0]):
        first = dest % 2 * half
        start = pl.multiple_of(order_ref[brow, dest // 2] * width, width)
        own = pl.ds(pl.multiple_of(first + side * fourth, fourth), fourth)
        out_ref[dest, :fourth, :] = feats_ref[own, pl.ds(start, width)]
        out_ref[dest, fourth:, : width // 2] = masked[first : first + fourth]
        out_ref[dest, fourth:, width // 2 :] = masked[first + fourth : first + half]


def step_kernel(
    own_ref,
    other_ref,
    left_mine_ref,
    left_other_ref,
    right_mine_ref,
    right_other_ref,
    moment_ref,
    second_ref,
    precond_ref,
    new_moment_ref,
    new_second_ref,
    sums_ref,
    grad_ref,
    left_ref,
    right_ref,
):
    half = own_ref.shape[0]
    quarter = half // 2
    side = lax.axis_index("c")
    part = lax.rem(lax.axis_index("zl"), 2)
    place = lambda i, n: pl.ds(pl.multiple_of(i * n, n), n)
    grad_ref[place(side, half), :] = own_ref[...]
    grad_ref[place(1 - side, half), :] = other_ref[...]
    left_ref[place(part, quarter), :] = left_mine_ref[...]
    left_ref[place(1 - part, quarter), :] = left_other_ref[...]
    right_ref[place(side, quarter), :] = right_mine_ref[...]
    right_ref[place(1 - side, quarter), :] = right_other_ref[...]
    tile = own_ref[:, place(part, half)]
    new_moment = 0.9 * moment_ref[...] + 0.1 * tile
    new_second = 0.95 * second_ref[...] + 0.05 * tile * tile
    new_moment_ref[...] = new_moment
    new_second_ref[...] = new_second
    direction = new_moment / (jnp.sqrt(new_second) + 1e-08)
    inner = dot_plain(split(left_ref[...]), split(grad_ref[...]))
    precond = dot_rows(split(inner), split(right_ref[...]))
    precond_ref[...] = precond
    lanes = lambda v: jnp.sum((v * v).reshape(-1, 8, 128), 0)
    sums_ref[0] = lanes(direction)
    sums_ref[1] = lanes(precond)


def scale_kernel(sums_ref, precond_ref, out_ref):
    total = jnp.sum(sums_ref[...], axis=0)
    across = lambda v: jnp.sum(jnp.sum(v, axis=1, keepdims=True), axis=0, keepdims=True)
    scale = jnp.sqrt(across(total[0:1]) / (across(total[1:2]) + 1e-06))
    out_ref[...] = scale * precond_ref[...]


def call(kernel, out_shape, in_specs, out_specs, scratch_shapes=()):
    return pl.pallas_call(
        kernel,
        out_shape=out_shape,
        in_specs=in_specs,
        out_specs=out_specs,
        scratch_shapes=scratch_shapes,
        compiler_params=pltpu.CompilerParams(vmem_limit_bytes=VMEM_LIMIT),
    )


VM = pl.BlockSpec(memory_space=pltpu.VMEM)
SM = pl.BlockSpec(memory_space=pltpu.SMEM)


def body(
    features,
    out_grads,
    token_counts,
    owner_order,
    moment,
    second,
    left_stat,
    right_stat,
    left_root,
    right_root,
):
    f32 = jnp.float32
    tok_rows = features.shape[0]
    block_size = left_stat.shape[-1]
    half_size = block_size // 2
    quarter = block_size // 4
    dests = 2 * features.shape[1] // block_size
    fourth = tok_rows // 4
    side_bit = lax.axis_index("c")
    part_bit = lax.axis_index("zl") % 2
    precise = lax.Precision.HIGH
    token_total = jnp.sum(token_counts).astype(f32)
    left_mine = left_root[0, 0]
    right_mine = right_root[0, 0]

    outgoing = call(
        pack_kernel,
        jax.ShapeDtypeStruct((dests, 2 * fourth, block_size), jnp.bfloat16),
        [SM, SM, VM, VM],
        VM,
    )(token_counts, owner_order, features, out_grads)
    left_other = partner(left_mine, "zl")
    right_other = partner(right_mine, "c")
    arrived = lax.all_to_all(outgoing, DP, split_axis=0, concat_axis=0, tiled=True)
    arrived, left_other, right_other = lax.optimization_barrier(
        (arrived, left_other, right_other)
    )
    feats_own = arrived[:, :fourth].reshape(-1, block_size)
    feats_other = partner(feats_own, "c")
    grads_low = arrived[:, fourth:, :half_size].reshape(-1, half_size)
    grads_high = arrived[:, fourth:, half_size:].reshape(-1, half_size)
    own_first = side_bit == 0
    grads_own = jnp.where(own_first, grads_low, grads_high)
    grads_other = jnp.where(own_first, grads_high, grads_low)
    partial = jnp.dot(grads_own.T, feats_own, preferred_element_type=f32) + jnp.dot(
        grads_other.T, feats_other, preferred_element_type=f32
    )
    own_half = (partial + partner(partial, "zl")) / token_total
    other_half = partner(own_half, "c")

    tile = jax.ShapeDtypeStruct((half_size, half_size), f32)
    precond, new_moment, new_second, sums = call(
        step_kernel,
        (tile, tile, tile, jax.ShapeDtypeStruct((2, 8, 128), f32)),
        [VM] * 8,
        (VM,) * 4,
        [
            pltpu.VMEM((block_size, block_size), f32),
            pltpu.VMEM((half_size, block_size), f32),
            pltpu.VMEM((half_size, block_size), f32),
        ],
    )(own_half, other_half, left_mine, left_other, right_mine, right_other, moment, second)

    sums = jnp.sum(sums, 1)
    sums = jnp.concatenate([sums, jnp.zeros((6, 128), f32)], 0)
    sums = jnp.sum(lax.all_gather(sums, "c"), 0)
    for axes in (("x", "y"), ("zh", "zl")):
        if axes[0] == "zh":
            sums = jnp.sum(sums, 0)
        copies = jnp.broadcast_to(sums, (lax.axis_size(axes), 8, 128))
        sums = lax.all_to_all(copies, axes, split_axis=0, concat_axis=0, tiled=True)
    update = call(scale_kernel, tile, [VM, VM], VM)(sums, precond)

    whole_block = jnp.where(
        own_first,
        jnp.concatenate([own_half, other_half], 0),
        jnp.concatenate([other_half, own_half], 0),
    )
    left_rows = lax.dynamic_slice_in_dim(own_half, part_bit * quarter, quarter, 0)
    right_cols = lax.dynamic_slice_in_dim(
        whole_block, part_bit * half_size + side_bit * quarter, quarter, 1
    )
    next_left = 0.95 * left_stat[0, 0] + 0.05 * (
        jnp.dot(left_rows, whole_block.T, precision=precise) / block_size
    )
    next_right = 0.95 * right_stat[0, 0] + 0.05 * (
        jnp.dot(right_cols.T, whole_block, precision=precise) / block_size
    )
    return (update, new_moment, new_second, next_left[None, None], next_right[None, None])


def solution(mesh):
    fine = Mesh(mesh.devices.reshape(SIZES), DP + SHARD)
    return jax.shard_map(
        body,
        mesh=fine,
        in_specs=(
            P(DP, None),
            P(DP, SHARD),
            P(),
            P(),
            P(SHARD, DP),
            P(SHARD, DP),
            P(SHARD, DP, None, None),
            P(SHARD, DP, None, None),
            P(SHARD, DP, None, None),
            P(SHARD, DP, None, None),
        ),
        out_specs=(
            P(SHARD, DP),
            P(SHARD, DP),
            P(SHARD, DP),
            P(SHARD, DP, None, None),
            P(SHARD, DP, None, None),
        ),
        check_vma=False,
    )
```

```python
import jax
import jax.numpy as jnp
from jax import lax
from jax.experimental import pallas as pl
from jax.experimental.pallas import tpu as pltpu
from jax.sharding import Mesh, PartitionSpec as P

DP = ("x", "zl")
SHARD = ("zh", "y", "c")
SIZES = (4, 4, 4, 8, 2)
VMEM_LIMIT = 40 * 1024 * 1024


def partner(value, axis):
    return lax.ppermute(value, axis, [(i, i ^ 1) for i in range(lax.axis_size(axis))])


def split(value):
    high = value.astype(jnp.bfloat16)
    return high, (value - high.astype(jnp.float32)).astype(jnp.bfloat16)


def dot_rows(a, b):
    dims = (((1,), (1,)), ((), ()))
    mul = lambda p, q: lax.dot_general(p, q, dims, preferred_element_type=jnp.float32)
    return mul(a[0], b[0]) + (mul(a[0], b[1]) + mul(a[1], b[0]))


def dot_plain(a, b):
    dims = (((1,), (0,)), ((), ()))
    mul = lambda p, q: lax.dot_general(p, q, dims, preferred_element_type=jnp.float32)
    return mul(a[0], b[0]) + (mul(a[0], b[1]) + mul(a[1], b[0]))


def z_partners():
    runs = SIZES[2]
    ahead = [((1, r), (2, r)) for r in range(runs)]
    ahead += [((3, r), (0, (r + 1) % runs)) for r in range(runs)]
    flat = lambda at: at[0] * runs + at[1]
    return [(flat(p), flat(q)) for p, q in ahead] + [(flat(q), flat(p)) for p, q in ahead]


def block_copies(order_ref, feats_ref, out_ref, sems, first, brow, column):
    half = feats_ref.shape[0] // 2
    width = out_ref.shape[2]
    own = pl.ds(pl.multiple_of(lax.axis_index("c") * half, half), half)
    return [
        pltpu.make_async_copy(
            feats_ref.at[own, pl.ds(pl.multiple_of(order_ref[x * 2 + column, brow] * width, width), width)],
            out_ref.at[x, pl.ds(first, half), :],
            sems.at[x],
        )
        for x in range(out_ref.shape[0])
    ]


def lend_kernel(order_ref, feats_ref, out_ref, sems):
    zl = lax.axis_index("zl")
    runs = lax.axis_size("zh")
    turn = jnp.where(zl == 3, 1, jnp.where(zl == 0, runs - 1, 0))
    brow = lax.rem(lax.axis_index("zh") + turn, runs) * lax.axis_size("y") + lax.axis_index("y")
    copies = block_copies(order_ref, feats_ref, out_ref, sems, 0, brow, 1 - zl // 2)
    for copy in copies:
        copy.start()
    for copy in copies:
        copy.wait()


def mask_kernel(counts_ref, grads_ref, out_ref):
    rows = lax.broadcasted_iota(jnp.int32, grads_ref.shape, 0)
    count = counts_ref[lax.axis_index("x") * lax.axis_size("zl") + lax.axis_index("zl")]
    masked = jnp.where(rows < count, grads_ref[...].astype(jnp.float32), 0.0)
    out_ref[...] = masked.astype(jnp.bfloat16)


def grads_copies(grads_ref, out_ref, sems, first):
    half = grads_ref.shape[0] // 2
    width = grads_ref.shape[1]
    return [
        pltpu.make_async_copy(
            grads_ref.at[pl.ds(half * part, half), :],
            out_ref.at[x, pl.ds(first, half), pl.ds(width * part, width)],
            sems.at[x, part],
        )
        for x in range(out_ref.shape[0])
        for part in range(2)
    ]


def own_kernel(order_ref, feats_ref, grads_ref, out_ref, sems, grads_sems):
    half = feats_ref.shape[0] // 2
    brow = lax.axis_index("zh") * lax.axis_size("y") + lax.axis_index("y")
    copies = block_copies(order_ref, feats_ref, out_ref, sems, 0, brow, lax.axis_index("zl") // 2)
    copies += grads_copies(grads_ref, out_ref, grads_sems, 2 * half)
    for copy in copies:
        copy.start()
    for copy in copies:
        copy.wait()


def lent_kernel(feats_ref, grads_ref, filled_ref, out_ref, sems, grads_sems):
    half = feats_ref.shape[1]
    copies = [
        pltpu.make_async_copy(feats_ref.at[x], out_ref.at[x, pl.ds(half, half), :], sems.at[x])
        for x in range(out_ref.shape[0])
    ]
    copies += grads_copies(grads_ref, out_ref, grads_sems, 3 * half)
    for copy in copies:
        copy.start()
    for copy in copies:
        copy.wait()


def roots_kernel(
    left_mine_ref,
    left_other_ref,
    right_mine_ref,
    right_other_ref,
    left_high_ref,
    left_low_ref,
    right_high_ref,
    right_low_ref,
):
    quarter = left_mine_ref.shape[0]
    side = lax.axis_index("c")
    part = lax.rem(lax.axis_index("zl"), 2)
    for bit, mine_ref, other_ref, high_ref, low_ref in (
        (part, left_mine_ref, left_other_ref, left_high_ref, left_low_ref),
        (side, right_mine_ref, right_other_ref, right_high_ref, right_low_ref),
    ):
        for place, ref in ((bit, mine_ref), (1 - bit, other_ref)):
            at = pl.ds(pl.multiple_of(place * quarter, quarter), quarter)
            high_ref[at, :], low_ref[at, :] = split(ref[...])


def lane_sums(value):
    squares = jnp.sum(value * value, axis=0, keepdims=True)
    return squares[:, :128] + squares[:, 128:]


def moment_kernel(own_ref, moment_ref, second_ref, new_moment_ref, new_second_ref, sum_ref):
    half = own_ref.shape[0]
    part = lax.rem(lax.axis_index("zl"), 2)
    tile = own_ref[:, pl.ds(pl.multiple_of(part * half, half), half)]
    new_moment = 0.9 * moment_ref[...] + 0.1 * tile
    new_second = 0.95 * second_ref[...] + 0.05 * tile * tile
    new_moment_ref[...] = new_moment
    new_second_ref[...] = new_second
    sum_ref[...] = lane_sums(new_moment / (jnp.sqrt(new_second) + 1e-08))


def step_kernel(
    own_ref,
    other_ref,
    left_high_ref,
    left_low_ref,
    right_high_ref,
    right_low_ref,
    sum_ref,
    precond_ref,
    sums_ref,
    high_ref,
    low_ref,
):
    half = own_ref.shape[0]
    side = lax.axis_index("c")
    for place, ref in ((side, own_ref), (1 - side, other_ref)):
        at = pl.ds(pl.multiple_of(place * half, half), half)
        high_ref[at, :], low_ref[at, :] = split(ref[...])
    inner = dot_plain((left_high_ref[...], left_low_ref[...]), (high_ref[...], low_ref[...]))
    precond = dot_rows(split(inner), (right_high_ref[...], right_low_ref[...]))
    precond_ref[...] = precond
    sums = jnp.concatenate([sum_ref[...], lane_sums(precond)], 0)
    sums_ref[...] = jnp.broadcast_to(sums[None], sums_ref.shape)


def scale_kernel(sums_ref, precond_ref, out_ref):
    total = jnp.sum(sums_ref[...], axis=0)
    across = lambda v: jnp.sum(jnp.sum(v, axis=1, keepdims=True), axis=0, keepdims=True)
    scale = jnp.sqrt(across(total[0:1]) / (across(total[1:2]) + 1e-06))
    out_ref[...] = scale * precond_ref[...]


def call(kernel, out_shape, in_specs, out_specs, scratch_shapes=(), aliases=None):
    return pl.pallas_call(
        kernel,
        out_shape=out_shape,
        in_specs=in_specs,
        out_specs=out_specs,
        scratch_shapes=scratch_shapes,
        input_output_aliases=aliases or {},
        compiler_params=pltpu.CompilerParams(vmem_limit_bytes=VMEM_LIMIT),
    )


VM = pl.BlockSpec(memory_space=pltpu.VMEM)
SM = pl.BlockSpec(memory_space=pltpu.SMEM)
ANY = pl.BlockSpec(memory_space=pl.ANY)


def body(
    features,
    out_grads,
    token_counts,
    owner_order,
    moment,
    second,
    left_stat,
    right_stat,
    left_root,
    right_root,
):
    f32 = jnp.float32
    tok_rows = features.shape[0]
    block_size = left_stat.shape[-1]
    half_size = block_size // 2
    quarter = block_size // 4
    side_bit = lax.axis_index("c")
    part_bit = lax.axis_index("zl") % 2
    precise = lax.Precision.HIGH
    token_total = jnp.sum(token_counts).astype(f32)
    left_mine = left_root[0, 0]
    right_mine = right_root[0, 0]

    half_rows = tok_rows // 2
    lines = lax.axis_size("x")
    order = owner_order.T
    lent = call(
        lend_kernel,
        jax.ShapeDtypeStruct((lines, half_rows, block_size), jnp.bfloat16),
        [SM, ANY],
        VM,
        [pltpu.SemaphoreType.DMA((lines,))],
    )(order, features)
    lent = lax.ppermute(lent, ("zl", "zh"), z_partners())
    masked = jax.ShapeDtypeStruct(out_grads.shape, jnp.bfloat16)
    grads = call(mask_kernel, masked, [SM, VM], VM)(token_counts, out_grads)
    lent_grads = lax.ppermute(grads, "zl", [(i, 3 - i) for i in range(4)])
    packed = jax.ShapeDtypeStruct((lines, 4 * half_rows, block_size), jnp.bfloat16)
    sems = [pltpu.SemaphoreType.DMA((lines,)), pltpu.SemaphoreType.DMA((lines, 2))]
    filled = call(own_kernel, packed, [SM, ANY, VM], ANY, sems)(order, features, grads)
    outgoing = call(lent_kernel, packed, [VM, VM, ANY], ANY, sems, {2: 0})(
        lent, lent_grads, filled
    )
    left_other = partner(left_mine, "zl")
    right_other = partner(right_mine, "c")
    arrived = lax.all_to_all(outgoing, "x", split_axis=0, concat_axis=0, tiled=True)
    root = jax.ShapeDtypeStruct((half_size, block_size), jnp.bfloat16)
    roots = call(roots_kernel, (root,) * 4, [VM] * 4, (VM,) * 4)(
        left_mine, left_other, right_mine, right_other
    )
    arrived, *roots = lax.optimization_barrier((arrived, *roots))
    feats_own = arrived[:, :tok_rows].reshape(-1, block_size)
    feats_other = partner(feats_own, "c")
    grads_low = arrived[:, tok_rows:, :half_size].reshape(-1, half_size)
    grads_high = arrived[:, tok_rows:, half_size:].reshape(-1, half_size)
    own_first = side_bit == 0
    grads_own = jnp.where(own_first, grads_low, grads_high)
    grads_other = jnp.where(own_first, grads_high, grads_low)
    partial = jnp.dot(grads_own.T, feats_own, preferred_element_type=f32) + jnp.dot(
        grads_other.T, feats_other, preferred_element_type=f32
    )
    own_half = (partial + partner(partial, "zl")) / token_total
    other_half = partner(own_half, "c")

    tile = jax.ShapeDtypeStruct((half_size, half_size), f32)
    new_moment, new_second, direction_sum = call(
        moment_kernel,
        (tile, tile, jax.ShapeDtypeStruct((1, 128), f32)),
        [VM] * 3,
        (VM,) * 3,
    )(own_half, moment, second)
    near = ("x", "y", "c")
    line = ("zl", "zh")
    precond, sums = call(
        step_kernel,
        (tile, jax.ShapeDtypeStruct((lax.axis_size(near), 2, 128), f32)),
        [VM] * 7,
        (VM,) * 2,
        [
            pltpu.VMEM((block_size, block_size), jnp.bfloat16),
            pltpu.VMEM((block_size, block_size), jnp.bfloat16),
        ],
    )(own_half, other_half, *roots, direction_sum)
    sums = lax.all_to_all(sums, near, split_axis=0, concat_axis=0, tiled=True)
    sums = jnp.broadcast_to(jnp.sum(sums, 0), (lax.axis_size(line), 2, 128))
    sums = lax.all_to_all(sums, line, split_axis=0, concat_axis=0, tiled=True)
    update = call(scale_kernel, tile, [VM, VM], VM)(sums, precond)

    whole_block = jnp.where(
        own_first,
        jnp.concatenate([own_half, other_half], 0),
        jnp.concatenate([other_half, own_half], 0),
    )
    left_rows = lax.dynamic_slice_in_dim(own_half, part_bit * quarter, quarter, 0)
    right_cols = lax.dynamic_slice_in_dim(
        whole_block, part_bit * half_size + side_bit * quarter, quarter, 1
    )
    next_left = 0.95 * left_stat[0, 0] + 0.05 * (
        jnp.dot(left_rows, whole_block.T, precision=precise) / block_size
    )
    next_right = 0.95 * right_stat[0, 0] + 0.05 * (
        jnp.dot(right_cols.T, whole_block, precision=precise) / block_size
    )
    return (update, new_moment, new_second, next_left[None, None], next_right[None, None])


def solution(mesh):
    fine = Mesh(mesh.devices.reshape(SIZES), DP + SHARD)
    return jax.shard_map(
        body,
        mesh=fine,
        in_specs=(
            P(DP, None),
            P(DP, SHARD),
            P(),
            P(),
            P(SHARD, DP),
            P(SHARD, DP),
            P(SHARD, DP, None, None),
            P(SHARD, DP, None, None),
            P(SHARD, DP, None, None),
            P(SHARD, DP, None, None),
        ),
        out_specs=(
            P(SHARD, DP),
            P(SHARD, DP),
            P(SHARD, DP),
            P(SHARD, DP, None, None),
            P(SHARD, DP, None, None),
        ),
        check_vma=False,
    )
```

```python
import jax
import jax.numpy as jnp
from jax import lax
from jax.experimental import pallas as pl
from jax.experimental.pallas import tpu as pltpu
from jax.sharding import Mesh, PartitionSpec as P

DP = ("x", "zl")
SHARD = ("zh", "y", "c")
SIZES = (4, 4, 4, 8, 2)
VMEM_LIMIT = 40 * 1024 * 1024


def partner(value, axis):
    return lax.ppermute(value, axis, [(i, i ^ 1) for i in range(lax.axis_size(axis))])


def split(value):
    high = value.astype(jnp.bfloat16)
    return high, (value - high.astype(jnp.float32)).astype(jnp.bfloat16)


def dot_rows(a, b):
    dims = (((1,), (1,)), ((), ()))
    mul = lambda p, q: lax.dot_general(p, q, dims, preferred_element_type=jnp.float32)
    return mul(a[0], b[0]) + (mul(a[0], b[1]) + mul(a[1], b[0]))


def dot_plain(a, b):
    dims = (((1,), (0,)), ((), ()))
    mul = lambda p, q: lax.dot_general(p, q, dims, preferred_element_type=jnp.float32)
    return mul(a[0], b[0]) + (mul(a[0], b[1]) + mul(a[1], b[0]))


def z_partners():
    runs = SIZES[2]
    ahead = [((1, r), (2, r)) for r in range(runs)]
    ahead += [((3, r), (0, (r + 1) % runs)) for r in range(runs)]
    flat = lambda at: at[0] * runs + at[1]
    return [(flat(p), flat(q)) for p, q in ahead] + [(flat(q), flat(p)) for p, q in ahead]


def block_copies(order_ref, feats_ref, out_ref, sems, first, brow, column):
    half = feats_ref.shape[0] // 2
    width = out_ref.shape[2]
    own = pl.ds(pl.multiple_of(lax.axis_index("c") * half, half), half)
    return [
        pltpu.make_async_copy(
            feats_ref.at[own, pl.ds(pl.multiple_of(order_ref[x * 2 + column, brow] * width, width), width)],
            out_ref.at[x, pl.ds(first, half), :],
            sems.at[x],
        )
        for x in range(out_ref.shape[0])
    ]


def lend_kernel(order_ref, feats_ref, out_ref, sems):
    zl = lax.axis_index("zl")
    runs = lax.axis_size("zh")
    turn = jnp.where(zl == 3, 1, jnp.where(zl == 0, runs - 1, 0))
    brow = lax.rem(lax.axis_index("zh") + turn, runs) * lax.axis_size("y") + lax.axis_index("y")
    copies = block_copies(order_ref, feats_ref, out_ref, sems, 0, brow, 1 - zl // 2)
    for copy in copies:
        copy.start()
    for copy in copies:
        copy.wait()


def mask_kernel(counts_ref, grads_ref, out_ref):
    rows = lax.broadcasted_iota(jnp.int32, grads_ref.shape, 0)
    count = counts_ref[lax.axis_index("x") * lax.axis_size("zl") + lax.axis_index("zl")]
    masked = jnp.where(rows < count, grads_ref[...].astype(jnp.float32), 0.0)
    out_ref[...] = masked.astype(jnp.bfloat16)


def grads_copies(grads_ref, out_ref, sems, first):
    half = grads_ref.shape[0] // 2
    width = grads_ref.shape[1]
    return [
        pltpu.make_async_copy(
            grads_ref.at[pl.ds(half * part, half), :],
            out_ref.at[x, pl.ds(first, half), pl.ds(width * part, width)],
            sems.at[x, part],
        )
        for x in range(out_ref.shape[0])
        for part in range(2)
    ]


def own_kernel(order_ref, feats_ref, grads_ref, out_ref, sems, grads_sems):
    half = feats_ref.shape[0] // 2
    brow = lax.axis_index("zh") * lax.axis_size("y") + lax.axis_index("y")
    copies = block_copies(order_ref, feats_ref, out_ref, sems, 0, brow, lax.axis_index("zl") // 2)
    copies += grads_copies(grads_ref, out_ref, grads_sems, 2 * half)
    for copy in copies:
        copy.start()
    for copy in copies:
        copy.wait()


def lent_kernel(feats_ref, grads_ref, filled_ref, out_ref, sems, grads_sems):
    half = feats_ref.shape[1]
    copies = [
        pltpu.make_async_copy(feats_ref.at[x], out_ref.at[x, pl.ds(half, half), :], sems.at[x])
        for x in range(out_ref.shape[0])
    ]
    copies += grads_copies(grads_ref, out_ref, grads_sems, 3 * half)
    for copy in copies:
        copy.start()
    for copy in copies:
        copy.wait()


def lane_sums(value):
    squares = jnp.sum(value * value, axis=0, keepdims=True)
    return squares[:, :128] + squares[:, 128:]


def moment_kernel(
    own_ref,
    moment_ref,
    second_ref,
    mine_ref,
    other_ref,
    new_moment_ref,
    new_second_ref,
    sum_ref,
    inner_ref,
    high_ref,
    low_ref,
    left_ref,
):
    half = own_ref.shape[0]
    quarter = half // 2
    side = lax.axis_index("c")
    part = lax.rem(lax.axis_index("zl"), 2)
    place = lambda i, n: pl.ds(pl.multiple_of(i * n, n), n)
    tile = own_ref[:, place(part, half)]
    new_moment = 0.9 * moment_ref[...] + 0.1 * tile
    new_second = 0.95 * second_ref[...] + 0.05 * tile * tile
    new_moment_ref[...] = new_moment
    new_second_ref[...] = new_second
    sum_ref[...] = lane_sums(new_moment / (jnp.sqrt(new_second) + 1e-08))
    left_ref[place(part, quarter), :] = mine_ref[...]
    left_ref[place(1 - part, quarter), :] = other_ref[...]
    inner_ref[...] = dot_plain(split(left_ref[:, place(side, half)]), split(own_ref[...]))
    high_ref[...], low_ref[...] = split(left_ref[:, place(1 - side, half)])


def step_kernel(
    inner_ref,
    other_ref,
    left_high_ref,
    left_low_ref,
    right_mine_ref,
    right_other_ref,
    sum_ref,
    precond_ref,
    sums_ref,
    right_ref,
):
    quarter = right_mine_ref.shape[0]
    side = lax.axis_index("c")
    place = lambda i, n: pl.ds(pl.multiple_of(i * n, n), n)
    right_ref[place(side, quarter), :] = right_mine_ref[...]
    right_ref[place(1 - side, quarter), :] = right_other_ref[...]
    left = (left_high_ref[...], left_low_ref[...])
    inner = inner_ref[...] + dot_plain(left, split(other_ref[...]))
    precond = dot_rows(split(inner), split(right_ref[...]))
    precond_ref[...] = precond
    sums = jnp.concatenate([sum_ref[...], lane_sums(precond)], 0)
    sums_ref[...] = jnp.broadcast_to(sums[None], sums_ref.shape)


def scale_kernel(sums_ref, precond_ref, out_ref):
    total = jnp.sum(sums_ref[...], axis=0)
    across = lambda v: jnp.sum(jnp.sum(v, axis=1, keepdims=True), axis=0, keepdims=True)
    scale = jnp.sqrt(across(total[0:1]) / (across(total[1:2]) + 1e-06))
    out_ref[...] = scale * precond_ref[...]


def call(kernel, out_shape, in_specs, out_specs, scratch_shapes=(), aliases=None):
    return pl.pallas_call(
        kernel,
        out_shape=out_shape,
        in_specs=in_specs,
        out_specs=out_specs,
        scratch_shapes=scratch_shapes,
        input_output_aliases=aliases or {},
        compiler_params=pltpu.CompilerParams(vmem_limit_bytes=VMEM_LIMIT),
    )


VM = pl.BlockSpec(memory_space=pltpu.VMEM)
SM = pl.BlockSpec(memory_space=pltpu.SMEM)
ANY = pl.BlockSpec(memory_space=pl.ANY)


def body(
    features,
    out_grads,
    token_counts,
    owner_order,
    moment,
    second,
    left_stat,
    right_stat,
    left_root,
    right_root,
):
    f32 = jnp.float32
    tok_rows = features.shape[0]
    block_size = left_stat.shape[-1]
    half_size = block_size // 2
    quarter = block_size // 4
    side_bit = lax.axis_index("c")
    part_bit = lax.axis_index("zl") % 2
    precise = lax.Precision.HIGH
    token_total = jnp.sum(token_counts).astype(f32)
    left_mine = left_root[0, 0]
    right_mine = right_root[0, 0]

    half_rows = tok_rows // 2
    lines = lax.axis_size("x")
    order = owner_order.T
    lent = call(
        lend_kernel,
        jax.ShapeDtypeStruct((lines, half_rows, block_size), jnp.bfloat16),
        [SM, ANY],
        VM,
        [pltpu.SemaphoreType.DMA((lines,))],
    )(order, features)
    lent = lax.ppermute(lent, ("zl", "zh"), z_partners())
    masked = jax.ShapeDtypeStruct(out_grads.shape, jnp.bfloat16)
    grads = call(mask_kernel, masked, [SM, VM], VM)(token_counts, out_grads)
    lent_grads = lax.ppermute(grads, "zl", [(i, 3 - i) for i in range(4)])
    packed = jax.ShapeDtypeStruct((lines, 4 * half_rows, block_size), jnp.bfloat16)
    sems = [pltpu.SemaphoreType.DMA((lines,)), pltpu.SemaphoreType.DMA((lines, 2))]
    filled = call(own_kernel, packed, [SM, ANY, VM], ANY, sems)(order, features, grads)
    outgoing = call(lent_kernel, packed, [VM, VM, ANY], ANY, sems, {2: 0})(
        lent, lent_grads, filled
    )
    left_other = partner(left_mine, "zl")
    right_other = partner(right_mine, "c")
    arrived = lax.all_to_all(outgoing, "x", split_axis=0, concat_axis=0, tiled=True)
    arrived, left_other, right_other = lax.optimization_barrier(
        (arrived, left_other, right_other)
    )
    feats_own = arrived[:, :tok_rows].reshape(-1, block_size)
    feats_other = partner(feats_own, "c")
    grads_low = arrived[:, tok_rows:, :half_size].reshape(-1, half_size)
    grads_high = arrived[:, tok_rows:, half_size:].reshape(-1, half_size)
    own_first = side_bit == 0
    grads_own = jnp.where(own_first, grads_low, grads_high)
    grads_other = jnp.where(own_first, grads_high, grads_low)
    partial = jnp.dot(grads_own.T, feats_own, preferred_element_type=f32) + jnp.dot(
        grads_other.T, feats_other, preferred_element_type=f32
    )
    own_half = (partial + partner(partial, "zl")) / token_total
    other_half = partner(own_half, "c")

    tile = jax.ShapeDtypeStruct((half_size, half_size), f32)
    piece = jax.ShapeDtypeStruct((half_size, half_size), jnp.bfloat16)
    rows = jax.ShapeDtypeStruct((half_size, block_size), f32)
    new_moment, new_second, direction_sum, inner, left_high, left_low = call(
        moment_kernel,
        (tile, tile, jax.ShapeDtypeStruct((1, 128), f32), rows, piece, piece),
        [VM] * 5,
        (VM,) * 6,
        [pltpu.VMEM(rows.shape, f32)],
    )(own_half, moment, second, left_mine, left_other)
    near = ("x", "y", "c")
    line = ("zl", "zh")
    precond, sums = call(
        step_kernel,
        (tile, jax.ShapeDtypeStruct((lax.axis_size(near), 2, 128), f32)),
        [VM] * 7,
        (VM,) * 2,
        [pltpu.VMEM(rows.shape, f32)],
    )(inner, other_half, left_high, left_low, right_mine, right_other, direction_sum)
    sums = lax.all_to_all(sums, near, split_axis=0, concat_axis=0, tiled=True)
    sums = jnp.broadcast_to(jnp.sum(sums, 0), (lax.axis_size(line), 2, 128))
    sums = lax.all_to_all(sums, line, split_axis=0, concat_axis=0, tiled=True)
    update = call(scale_kernel, tile, [VM, VM], VM)(sums, precond)

    whole_block = jnp.where(
        own_first,
        jnp.concatenate([own_half, other_half], 0),
        jnp.concatenate([other_half, own_half], 0),
    )
    left_rows = lax.dynamic_slice_in_dim(own_half, part_bit * quarter, quarter, 0)
    right_cols = lax.dynamic_slice_in_dim(
        whole_block, part_bit * half_size + side_bit * quarter, quarter, 1
    )
    next_left = 0.95 * left_stat[0, 0] + 0.05 * (
        jnp.dot(left_rows, whole_block.T, precision=precise) / block_size
    )
    next_right = 0.95 * right_stat[0, 0] + 0.05 * (
        jnp.dot(right_cols.T, whole_block, precision=precise) / block_size
    )
    return (update, new_moment, new_second, next_left[None, None], next_right[None, None])


def solution(mesh):
    fine = Mesh(mesh.devices.reshape(SIZES), DP + SHARD)
    return jax.shard_map(
        body,
        mesh=fine,
        in_specs=(
            P(DP, None),
            P(DP, SHARD),
            P(),
            P(),
            P(SHARD, DP),
            P(SHARD, DP),
            P(SHARD, DP, None, None),
            P(SHARD, DP, None, None),
            P(SHARD, DP, None, None),
            P(SHARD, DP, None, None),
        ),
        out_specs=(
            P(SHARD, DP),
            P(SHARD, DP),
            P(SHARD, DP),
            P(SHARD, DP, None, None),
            P(SHARD, DP, None, None),
        ),
        check_vma=False,
    )
```

```python
import jax
import jax.numpy as jnp
from jax import lax
from jax.experimental import pallas as pl
from jax.experimental.pallas import tpu as pltpu
from jax.sharding import Mesh, PartitionSpec as P

DP = ("x", "zl")
SHARD = ("zh", "y", "c")
SIZES = (4, 4, 4, 8, 2)
VMEM_LIMIT = 40 * 1024 * 1024


def partner(value, axis):
    return lax.ppermute(value, axis, [(i, i ^ 1) for i in range(lax.axis_size(axis))])


def split(value):
    high = value.astype(jnp.bfloat16)
    return high, (value - high.astype(jnp.float32)).astype(jnp.bfloat16)


def dot_rows(a, b):
    dims = (((1,), (1,)), ((), ()))
    mul = lambda p, q: lax.dot_general(p, q, dims, preferred_element_type=jnp.float32)
    return mul(a[0], b[0]) + (mul(a[0], b[1]) + mul(a[1], b[0]))


def dot_plain(a, b):
    dims = (((1,), (0,)), ((), ()))
    mul = lambda p, q: lax.dot_general(p, q, dims, preferred_element_type=jnp.float32)
    return mul(a[0], b[0]) + (mul(a[0], b[1]) + mul(a[1], b[0]))


def z_partners():
    runs = SIZES[2]
    ahead = [((1, r), (2, r)) for r in range(runs)]
    ahead += [((3, r), (0, (r + 1) % runs)) for r in range(runs)]
    flat = lambda at: at[0] * runs + at[1]
    return [(flat(p), flat(q)) for p, q in ahead] + [(flat(q), flat(p)) for p, q in ahead]


def block_copies(order_ref, feats_ref, out_ref, sems, first, brow, column):
    half = feats_ref.shape[0] // 2
    width = out_ref.shape[2]
    own = pl.ds(pl.multiple_of(lax.axis_index("c") * half, half), half)
    return [
        pltpu.make_async_copy(
            feats_ref.at[own, pl.ds(pl.multiple_of(order_ref[x * 2 + column, brow] * width, width), width)],
            out_ref.at[x, pl.ds(first, half), :],
            sems.at[x],
        )
        for x in range(out_ref.shape[0])
    ]


def lend_kernel(order_ref, feats_ref, out_ref, sems):
    zl = lax.axis_index("zl")
    runs = lax.axis_size("zh")
    turn = jnp.where(zl == 3, 1, jnp.where(zl == 0, runs - 1, 0))
    brow = lax.rem(lax.axis_index("zh") + turn, runs) * lax.axis_size("y") + lax.axis_index("y")
    copies = block_copies(order_ref, feats_ref, out_ref, sems, 0, brow, 1 - zl // 2)
    for copy in copies:
        copy.start()
    for copy in copies:
        copy.wait()


def mask_kernel(counts_ref, grads_ref, out_ref):
    rows = lax.broadcasted_iota(jnp.int32, grads_ref.shape, 0)
    count = counts_ref[lax.axis_index("x") * lax.axis_size("zl") + lax.axis_index("zl")]
    masked = jnp.where(rows < count, grads_ref[...].astype(jnp.float32), 0.0)
    out_ref[...] = masked.astype(jnp.bfloat16)


def grads_copies(grads_ref, out_ref, sems, first):
    half = grads_ref.shape[0] // 2
    width = grads_ref.shape[1]
    return [
        pltpu.make_async_copy(
            grads_ref.at[pl.ds(half * part, half), :],
            out_ref.at[x, pl.ds(first, half), pl.ds(width * part, width)],
            sems.at[x, part],
        )
        for x in range(out_ref.shape[0])
        for part in range(2)
    ]


def own_kernel(order_ref, feats_ref, grads_ref, out_ref, sems, grads_sems):
    half = feats_ref.shape[0] // 2
    brow = lax.axis_index("zh") * lax.axis_size("y") + lax.axis_index("y")
    copies = block_copies(order_ref, feats_ref, out_ref, sems, 0, brow, lax.axis_index("zl") // 2)
    copies += grads_copies(grads_ref, out_ref, grads_sems, 2 * half)
    for copy in copies:
        copy.start()
    for copy in copies:
        copy.wait()


def lent_kernel(feats_ref, grads_ref, filled_ref, out_ref, sems, grads_sems):
    half = feats_ref.shape[1]
    copies = [
        pltpu.make_async_copy(feats_ref.at[x], out_ref.at[x, pl.ds(half, half), :], sems.at[x])
        for x in range(out_ref.shape[0])
    ]
    copies += grads_copies(grads_ref, out_ref, grads_sems, 3 * half)
    for copy in copies:
        copy.start()
    for copy in copies:
        copy.wait()


def lane_sums(value):
    squares = jnp.sum(value * value, axis=0, keepdims=True)
    return squares[:, :128] + squares[:, 128:]


def moment_kernel(
    own_ref,
    moment_ref,
    second_ref,
    mine_ref,
    other_ref,
    new_moment_ref,
    new_second_ref,
    sum_ref,
    inner_ref,
    high_ref,
    low_ref,
    left_ref,
):
    half = own_ref.shape[0]
    quarter = half // 2
    side = lax.axis_index("c")
    part = lax.rem(lax.axis_index("zl"), 2)
    place = lambda i, n: pl.ds(pl.multiple_of(i * n, n), n)
    tile = own_ref[:, place(part, half)]
    new_moment = 0.9 * moment_ref[...] + 0.1 * tile
    new_second = 0.95 * second_ref[...] + 0.05 * tile * tile
    new_moment_ref[...] = new_moment
    new_second_ref[...] = new_second
    sum_ref[...] = lane_sums(new_moment / (jnp.sqrt(new_second) + 1e-08))
    left_ref[place(part, quarter), :] = mine_ref[...]
    left_ref[place(1 - part, quarter), :] = other_ref[...]
    inner_ref[...] = dot_plain(split(left_ref[:, place(side, half)]), split(own_ref[...]))
    high_ref[...], low_ref[...] = split(left_ref[:, place(1 - side, half)])


def step_kernel(
    inner_ref,
    other_ref,
    left_high_ref,
    left_low_ref,
    right_mine_ref,
    right_other_ref,
    sum_ref,
    precond_ref,
    sums_ref,
    right_ref,
):
    quarter = right_mine_ref.shape[0]
    side = lax.axis_index("c")
    place = lambda i, n: pl.ds(pl.multiple_of(i * n, n), n)
    right_ref[place(side, quarter), :] = right_mine_ref[...]
    right_ref[place(1 - side, quarter), :] = right_other_ref[...]
    left = (left_high_ref[...], left_low_ref[...])
    inner = inner_ref[...] + dot_plain(left, split(other_ref[...]))
    precond = dot_rows(split(inner), split(right_ref[...]))
    precond_ref[...] = precond
    sums = jnp.concatenate([sum_ref[...], lane_sums(precond)], 0)
    sums_ref[...] = jnp.broadcast_to(sums[None], sums_ref.shape)


def scale_kernel(sums_ref, precond_ref, out_ref):
    total = jnp.sum(sums_ref[...], axis=0)
    across = lambda v: jnp.sum(jnp.sum(v, axis=1, keepdims=True), axis=0, keepdims=True)
    scale = jnp.sqrt(across(total[0:1]) / (across(total[1:2]) + 1e-06))
    out_ref[...] = scale * precond_ref[...]


def call(kernel, out_shape, in_specs, out_specs, scratch_shapes=(), aliases=None):
    return pl.pallas_call(
        kernel,
        out_shape=out_shape,
        in_specs=in_specs,
        out_specs=out_specs,
        scratch_shapes=scratch_shapes,
        input_output_aliases=aliases or {},
        compiler_params=pltpu.CompilerParams(vmem_limit_bytes=VMEM_LIMIT),
    )


VM = pl.BlockSpec(memory_space=pltpu.VMEM)
SM = pl.BlockSpec(memory_space=pltpu.SMEM)
ANY = pl.BlockSpec(memory_space=pl.ANY)


def body(
    features,
    out_grads,
    token_counts,
    owner_order,
    moment,
    second,
    left_stat,
    right_stat,
    left_root,
    right_root,
):
    f32 = jnp.float32
    tok_rows = features.shape[0]
    block_size = left_stat.shape[-1]
    half_size = block_size // 2
    quarter = block_size // 4
    side_bit = lax.axis_index("c")
    part_bit = lax.axis_index("zl") % 2
    precise = lax.Precision.HIGH
    token_total = jnp.sum(token_counts).astype(f32)
    left_mine = left_root[0, 0]
    right_mine = right_root[0, 0]

    half_rows = tok_rows // 2
    lines = lax.axis_size("x")
    order = owner_order.T
    lent = call(
        lend_kernel,
        jax.ShapeDtypeStruct((lines, half_rows, block_size), jnp.bfloat16),
        [SM, ANY],
        VM,
        [pltpu.SemaphoreType.DMA((lines,))],
    )(order, features)
    lent = lax.ppermute(lent, ("zl", "zh"), z_partners())
    masked = jax.ShapeDtypeStruct(out_grads.shape, jnp.bfloat16)
    grads = call(mask_kernel, masked, [SM, VM], VM)(token_counts, out_grads)
    lent_grads = lax.ppermute(grads, "zl", [(i, 3 - i) for i in range(4)])
    packed = jax.ShapeDtypeStruct((lines, 4 * half_rows, block_size), jnp.bfloat16)
    sems = [pltpu.SemaphoreType.DMA((lines,)), pltpu.SemaphoreType.DMA((lines, 2))]
    filled = call(own_kernel, packed, [SM, ANY, VM], ANY, sems)(order, features, grads)
    outgoing = call(lent_kernel, packed, [VM, VM, ANY], ANY, sems, {2: 0})(
        lent, lent_grads, filled
    )
    left_other = partner(left_mine, "zl")
    right_other = partner(right_mine, "c")
    arrived = lax.all_to_all(outgoing, "x", split_axis=0, concat_axis=0, tiled=True)
    arrived, left_other, right_other = lax.optimization_barrier(
        (arrived, left_other, right_other)
    )
    feats_own = arrived[:, :tok_rows].reshape(-1, block_size)
    feats_other = partner(feats_own, "c")
    grads_low = arrived[:, tok_rows:, :half_size].reshape(-1, half_size)
    grads_high = arrived[:, tok_rows:, half_size:].reshape(-1, half_size)
    own_first = side_bit == 0
    grads_own = jnp.where(own_first, grads_low, grads_high)
    grads_other = jnp.where(own_first, grads_high, grads_low)
    partial = jnp.dot(grads_own.T, feats_own, preferred_element_type=f32) + jnp.dot(
        grads_other.T, feats_other, preferred_element_type=f32
    )
    own_half = (partial + partner(partial, "zl")) / token_total
    other_half = partner(own_half, "c")

    tile = jax.ShapeDtypeStruct((half_size, half_size), f32)
    piece = jax.ShapeDtypeStruct((half_size, half_size), jnp.bfloat16)
    rows = jax.ShapeDtypeStruct((half_size, block_size), f32)
    new_moment, new_second, direction_sum, inner, left_high, left_low = call(
        moment_kernel,
        (tile, tile, jax.ShapeDtypeStruct((1, 128), f32), rows, piece, piece),
        [VM] * 5,
        (VM,) * 6,
        [pltpu.VMEM(rows.shape, f32)],
    )(own_half, moment, second, left_mine, left_other)
    near = ("x", "y", "c")
    line = ("zl", "zh")
    precond, sums = call(
        step_kernel,
        (tile, jax.ShapeDtypeStruct((lax.axis_size(near), 2, 128), f32)),
        [VM] * 7,
        (VM,) * 2,
        [pltpu.VMEM(rows.shape, f32)],
    )(inner, other_half, left_high, left_low, right_mine, right_other, direction_sum)
    sums = lax.all_to_all(sums, near, split_axis=0, concat_axis=0, tiled=True)
    sums, own_rows, other_rows = lax.optimization_barrier((sums, own_half, other_half))
    sums = jnp.broadcast_to(jnp.sum(sums, 0), (lax.axis_size(line), 2, 128))
    sums = lax.all_to_all(sums, line, split_axis=0, concat_axis=0, tiled=True)
    update = call(scale_kernel, tile, [VM, VM], VM)(sums, precond)

    whole_block = jnp.where(
        own_first,
        jnp.concatenate([own_rows, other_rows], 0),
        jnp.concatenate([other_rows, own_rows], 0),
    )
    left_rows = lax.dynamic_slice_in_dim(own_rows, part_bit * quarter, quarter, 0)
    right_cols = lax.dynamic_slice_in_dim(
        whole_block, part_bit * half_size + side_bit * quarter, quarter, 1
    )
    next_left = 0.95 * left_stat[0, 0] + 0.05 * (
        jnp.dot(left_rows, whole_block.T, precision=precise) / block_size
    )
    next_right = 0.95 * right_stat[0, 0] + 0.05 * (
        jnp.dot(right_cols.T, whole_block, precision=precise) / block_size
    )
    return (update, new_moment, new_second, next_left[None, None], next_right[None, None])


def solution(mesh):
    fine = Mesh(mesh.devices.reshape(SIZES), DP + SHARD)
    return jax.shard_map(
        body,
        mesh=fine,
        in_specs=(
            P(DP, None),
            P(DP, SHARD),
            P(),
            P(),
            P(SHARD, DP),
            P(SHARD, DP),
            P(SHARD, DP, None, None),
            P(SHARD, DP, None, None),
            P(SHARD, DP, None, None),
            P(SHARD, DP, None, None),
        ),
        out_specs=(
            P(SHARD, DP),
            P(SHARD, DP),
            P(SHARD, DP),
            P(SHARD, DP, None, None),
            P(SHARD, DP, None, None),
        ),
        check_vma=False,
    )
```

```python
import jax
import jax.numpy as jnp
from jax import lax
from jax.experimental import pallas as pl
from jax.experimental.pallas import tpu as pltpu
from jax.sharding import Mesh, PartitionSpec as P

DP = ("x", "zl")
SHARD = ("zh", "y", "c")
SIZES = (4, 4, 4, 8, 2)
VMEM_LIMIT = 40 * 1024 * 1024


def partner(value, axis):
    return lax.ppermute(value, axis, [(i, i ^ 1) for i in range(lax.axis_size(axis))])


def split(value):
    high = value.astype(jnp.bfloat16)
    return high, (value - high.astype(jnp.float32)).astype(jnp.bfloat16)


def dot_rows(a, b):
    dims = (((1,), (1,)), ((), ()))
    mul = lambda p, q: lax.dot_general(p, q, dims, preferred_element_type=jnp.float32)
    return mul(a[0], b[0]) + (mul(a[0], b[1]) + mul(a[1], b[0]))


def dot_plain(a, b):
    dims = (((1,), (0,)), ((), ()))
    mul = lambda p, q: lax.dot_general(p, q, dims, preferred_element_type=jnp.float32)
    return mul(a[0], b[0]) + (mul(a[0], b[1]) + mul(a[1], b[0]))


def z_partners():
    runs = SIZES[2]
    ahead = [((1, r), (2, r)) for r in range(runs)]
    ahead += [((3, r), (0, (r + 1) % runs)) for r in range(runs)]
    flat = lambda at: at[0] * runs + at[1]
    return [(flat(p), flat(q)) for p, q in ahead] + [(flat(q), flat(p)) for p, q in ahead]


def block_copies(order_ref, feats_ref, out_ref, sems, first, brow, column):
    half = feats_ref.shape[0] // 2
    width = out_ref.shape[2]
    own = pl.ds(pl.multiple_of(lax.axis_index("c") * half, half), half)
    return [
        pltpu.make_async_copy(
            feats_ref.at[own, pl.ds(pl.multiple_of(order_ref[x * 2 + column, brow] * width, width), width)],
            out_ref.at[x, pl.ds(first, half), :],
            sems.at[x],
        )
        for x in range(out_ref.shape[0])
    ]


def lend_kernel(order_ref, feats_ref, after_ref, out_ref, sems):
    zl = lax.axis_index("zl")
    runs = lax.axis_size("zh")
    turn = jnp.where(zl == 3, 1, jnp.where(zl == 0, runs - 1, 0))
    brow = lax.rem(lax.axis_index("zh") + turn, runs) * lax.axis_size("y") + lax.axis_index("y")
    copies = block_copies(order_ref, feats_ref, out_ref, sems, 0, brow, 1 - zl // 2)
    for copy in copies:
        copy.start()
    for copy in copies:
        copy.wait()


def masked_rows(counts_ref, grads_ref, zl):
    rows = lax.broadcasted_iota(jnp.int32, grads_ref.shape, 0)
    count = counts_ref[lax.axis_index("x") * lax.axis_size("zl") + zl]
    masked = jnp.where(rows < count, grads_ref[...].astype(jnp.float32), 0.0)
    return masked.astype(jnp.bfloat16)


def grads_copies(grads_ref, out_ref, sems, first):
    half = grads_ref.shape[0] // 2
    width = grads_ref.shape[1]
    return [
        pltpu.make_async_copy(
            grads_ref.at[pl.ds(half * part, half), :],
            out_ref.at[x, pl.ds(first, half), pl.ds(width * part, width)],
            sems.at[x, part],
        )
        for x in range(out_ref.shape[0])
        for part in range(2)
    ]


def own_kernel(
    counts_ref,
    order_ref,
    feats_ref,
    grads_ref,
    lent_grads_ref,
    out_ref,
    own_ref,
    lent_ref,
    sems,
    own_sems,
    lent_sems,
):
    half = feats_ref.shape[0] // 2
    zl = lax.axis_index("zl")
    brow = lax.axis_index("zh") * lax.axis_size("y") + lax.axis_index("y")
    copies = block_copies(order_ref, feats_ref, out_ref, sems, 0, brow, zl // 2)
    for copy in copies:
        copy.start()
    own_ref[...] = masked_rows(counts_ref, grads_ref, zl)
    lent_ref[...] = masked_rows(counts_ref, lent_grads_ref, 3 - zl)
    others = grads_copies(own_ref, out_ref, own_sems, 2 * half)
    others += grads_copies(lent_ref, out_ref, lent_sems, 3 * half)
    for copy in others:
        copy.start()
    for copy in copies + others:
        copy.wait()


def lent_kernel(feats_ref, filled_ref, out_ref, sems):
    half = feats_ref.shape[1]
    copies = [
        pltpu.make_async_copy(feats_ref.at[x], out_ref.at[x, pl.ds(half, half), :], sems.at[x])
        for x in range(out_ref.shape[0])
    ]
    for copy in copies:
        copy.start()
    for copy in copies:
        copy.wait()


def lane_sums(value):
    squares = jnp.sum(value * value, axis=0, keepdims=True)
    return squares[:, :128] + squares[:, 128:]


def moment_kernel(
    own_ref,
    moment_ref,
    second_ref,
    mine_ref,
    other_ref,
    new_moment_ref,
    new_second_ref,
    sum_ref,
    inner_ref,
    high_ref,
    low_ref,
    left_ref,
):
    half = own_ref.shape[0]
    quarter = half // 2
    side = lax.axis_index("c")
    part = lax.rem(lax.axis_index("zl"), 2)
    place = lambda i, n: pl.ds(pl.multiple_of(i * n, n), n)
    tile = own_ref[:, place(part, half)]
    new_moment = 0.9 * moment_ref[...] + 0.1 * tile
    new_second = 0.95 * second_ref[...] + 0.05 * tile * tile
    new_moment_ref[...] = new_moment
    new_second_ref[...] = new_second
    sum_ref[...] = lane_sums(new_moment / (jnp.sqrt(new_second) + 1e-08))
    left_ref[place(part, quarter), :] = mine_ref[...]
    left_ref[place(1 - part, quarter), :] = other_ref[...]
    inner_ref[...] = dot_plain(split(left_ref[:, place(side, half)]), split(own_ref[...]))
    high_ref[...], low_ref[...] = split(left_ref[:, place(1 - side, half)])


def step_kernel(
    inner_ref,
    other_ref,
    left_high_ref,
    left_low_ref,
    right_mine_ref,
    right_other_ref,
    sum_ref,
    precond_ref,
    sums_ref,
    right_ref,
):
    quarter = right_mine_ref.shape[0]
    side = lax.axis_index("c")
    place = lambda i, n: pl.ds(pl.multiple_of(i * n, n), n)
    right_ref[place(side, quarter), :] = right_mine_ref[...]
    right_ref[place(1 - side, quarter), :] = right_other_ref[...]
    left = (left_high_ref[...], left_low_ref[...])
    inner = inner_ref[...] + dot_plain(left, split(other_ref[...]))
    precond = dot_rows(split(inner), split(right_ref[...]))
    precond_ref[...] = precond
    sums = jnp.concatenate([sum_ref[...], lane_sums(precond)], 0)
    sums_ref[...] = jnp.broadcast_to(sums[None], sums_ref.shape)


def scale_kernel(sums_ref, precond_ref, out_ref):
    total = jnp.sum(sums_ref[...], axis=0)
    across = lambda v: jnp.sum(jnp.sum(v, axis=1, keepdims=True), axis=0, keepdims=True)
    scale = jnp.sqrt(across(total[0:1]) / (across(total[1:2]) + 1e-06))
    out_ref[...] = scale * precond_ref[...]


def call(kernel, out_shape, in_specs, out_specs, scratch_shapes=(), aliases=None):
    return pl.pallas_call(
        kernel,
        out_shape=out_shape,
        in_specs=in_specs,
        out_specs=out_specs,
        scratch_shapes=scratch_shapes,
        input_output_aliases=aliases or {},
        compiler_params=pltpu.CompilerParams(vmem_limit_bytes=VMEM_LIMIT),
    )


VM = pl.BlockSpec(memory_space=pltpu.VMEM)
SM = pl.BlockSpec(memory_space=pltpu.SMEM)
ANY = pl.BlockSpec(memory_space=pl.ANY)


def body(
    features,
    out_grads,
    token_counts,
    owner_order,
    moment,
    second,
    left_stat,
    right_stat,
    left_root,
    right_root,
):
    f32 = jnp.float32
    tok_rows = features.shape[0]
    block_size = left_stat.shape[-1]
    half_size = block_size // 2
    quarter = block_size // 4
    side_bit = lax.axis_index("c")
    part_bit = lax.axis_index("zl") % 2
    precise = lax.Precision.HIGH
    token_total = jnp.sum(token_counts).astype(f32)
    left_mine = left_root[0, 0]
    right_mine = right_root[0, 0]

    half_rows = tok_rows // 2
    lines = lax.axis_size("x")
    order = owner_order.T
    lent_grads = lax.ppermute(out_grads, "zl", [(i, 3 - i) for i in range(4)])
    lent = call(
        lend_kernel,
        jax.ShapeDtypeStruct((lines, half_rows, block_size), jnp.bfloat16),
        [SM, ANY, ANY],
        VM,
        [pltpu.SemaphoreType.DMA((lines,))],
    )(order, features, lent_grads)
    lent = lax.ppermute(lent, ("zl", "zh"), z_partners())
    packed = jax.ShapeDtypeStruct((lines, 4 * half_rows, block_size), jnp.bfloat16)
    buffer = pltpu.VMEM(out_grads.shape, jnp.bfloat16)
    each, pairs = pltpu.SemaphoreType.DMA((lines,)), pltpu.SemaphoreType.DMA((lines, 2))
    filled = call(
        own_kernel, packed, [SM, SM, ANY, VM, VM], ANY, [buffer, buffer, each, pairs, pairs]
    )(token_counts, order, features, out_grads, lent_grads)
    outgoing = call(lent_kernel, packed, [VM, ANY], ANY, [each], {1: 0})(lent, filled)
    left_other = partner(left_mine, "zl")
    right_other = partner(right_mine, "c")
    arrived = lax.all_to_all(outgoing, "x", split_axis=0, concat_axis=0, tiled=True)
    arrived, left_other, right_other = lax.optimization_barrier(
        (arrived, left_other, right_other)
    )
    feats_own = arrived[:, :tok_rows].reshape(-1, block_size)
    feats_other = partner(feats_own, "c")
    grads_low = arrived[:, tok_rows:, :half_size].reshape(-1, half_size)
    grads_high = arrived[:, tok_rows:, half_size:].reshape(-1, half_size)
    own_first = side_bit == 0
    grads_own = jnp.where(own_first, grads_low, grads_high)
    grads_other = jnp.where(own_first, grads_high, grads_low)
    partial = jnp.dot(grads_own.T, feats_own, preferred_element_type=f32) + jnp.dot(
        grads_other.T, feats_other, preferred_element_type=f32
    )
    own_half = (partial + partner(partial, "zl")) / token_total
    other_half = partner(own_half, "c")

    tile = jax.ShapeDtypeStruct((half_size, half_size), f32)
    piece = jax.ShapeDtypeStruct((half_size, half_size), jnp.bfloat16)
    rows = jax.ShapeDtypeStruct((half_size, block_size), f32)
    new_moment, new_second, direction_sum, inner, left_high, left_low = call(
        moment_kernel,
        (tile, tile, jax.ShapeDtypeStruct((1, 128), f32), rows, piece, piece),
        [VM] * 5,
        (VM,) * 6,
        [pltpu.VMEM(rows.shape, f32)],
    )(own_half, moment, second, left_mine, left_other)
    near = ("x", "y", "c")
    line = ("zl", "zh")
    precond, sums = call(
        step_kernel,
        (tile, jax.ShapeDtypeStruct((lax.axis_size(near), 2, 128), f32)),
        [VM] * 7,
        (VM,) * 2,
        [pltpu.VMEM(rows.shape, f32)],
    )(inner, other_half, left_high, left_low, right_mine, right_other, direction_sum)
    sums = lax.all_to_all(sums, near, split_axis=0, concat_axis=0, tiled=True)
    sums, own_rows, other_rows = lax.optimization_barrier((sums, own_half, other_half))
    sums = jnp.broadcast_to(jnp.sum(sums, 0), (lax.axis_size(line), 2, 128))
    sums = lax.all_to_all(sums, line, split_axis=0, concat_axis=0, tiled=True)
    update = call(scale_kernel, tile, [VM, VM], VM)(sums, precond)

    whole_block = jnp.where(
        own_first,
        jnp.concatenate([own_rows, other_rows], 0),
        jnp.concatenate([other_rows, own_rows], 0),
    )
    left_rows = lax.dynamic_slice_in_dim(own_rows, part_bit * quarter, quarter, 0)
    right_cols = lax.dynamic_slice_in_dim(
        whole_block, part_bit * half_size + side_bit * quarter, quarter, 1
    )
    next_left = 0.95 * left_stat[0, 0] + 0.05 * (
        jnp.dot(left_rows, whole_block.T, precision=precise) / block_size
    )
    next_right = 0.95 * right_stat[0, 0] + 0.05 * (
        jnp.dot(right_cols.T, whole_block, precision=precise) / block_size
    )
    return (update, new_moment, new_second, next_left[None, None], next_right[None, None])


def solution(mesh):
    fine = Mesh(mesh.devices.reshape(SIZES), DP + SHARD)
    return jax.shard_map(
        body,
        mesh=fine,
        in_specs=(
            P(DP, None),
            P(DP, SHARD),
            P(),
            P(),
            P(SHARD, DP),
            P(SHARD, DP),
            P(SHARD, DP, None, None),
            P(SHARD, DP, None, None),
            P(SHARD, DP, None, None),
            P(SHARD, DP, None, None),
        ),
        out_specs=(
            P(SHARD, DP),
            P(SHARD, DP),
            P(SHARD, DP),
            P(SHARD, DP, None, None),
            P(SHARD, DP, None, None),
        ),
        check_vma=False,
    )
```

```python
import jax
import jax.numpy as jnp
from jax import lax
from jax.experimental import pallas as pl
from jax.experimental.pallas import tpu as pltpu
from jax.sharding import Mesh, PartitionSpec as P

DP = ("x", "zl")
SHARD = ("zh", "y", "c")
SIZES = (4, 4, 4, 8, 2)
VMEM_LIMIT = 40 * 1024 * 1024


def partner(value, axis):
    return lax.ppermute(value, axis, [(i, i ^ 1) for i in range(lax.axis_size(axis))])


def split(value):
    high = value.astype(jnp.bfloat16)
    return high, (value - high.astype(jnp.float32)).astype(jnp.bfloat16)


def dot_rows(a, b):
    dims = (((1,), (1,)), ((), ()))
    mul = lambda p, q: lax.dot_general(p, q, dims, preferred_element_type=jnp.float32)
    return mul(a[0], b[0]) + (mul(a[0], b[1]) + mul(a[1], b[0]))


def dot_plain(a, b):
    dims = (((1,), (0,)), ((), ()))
    mul = lambda p, q: lax.dot_general(p, q, dims, preferred_element_type=jnp.float32)
    return mul(a[0], b[0]) + (mul(a[0], b[1]) + mul(a[1], b[0]))


def z_partners():
    runs = SIZES[2]
    ahead = [((1, r), (2, r)) for r in range(runs)]
    ahead += [((3, r), (0, (r + 1) % runs)) for r in range(runs)]
    flat = lambda at: at[0] * runs + at[1]
    return [(flat(p), flat(q)) for p, q in ahead] + [(flat(q), flat(p)) for p, q in ahead]


def block_copies(order_ref, feats_ref, out_ref, sems, first, brow, column):
    half = feats_ref.shape[0] // 2
    width = out_ref.shape[2]
    own = pl.ds(pl.multiple_of(lax.axis_index("c") * half, half), half)
    return [
        pltpu.make_async_copy(
            feats_ref.at[own, pl.ds(pl.multiple_of(order_ref[x * 2 + column, brow] * width, width), width)],
            out_ref.at[x, pl.ds(first, half), :],
            sems.at[x],
        )
        for x in range(out_ref.shape[0])
    ]


def lend_kernel(order_ref, feats_ref, out_ref, sems):
    zl = lax.axis_index("zl")
    runs = lax.axis_size("zh")
    turn = jnp.where(zl == 3, 1, jnp.where(zl == 0, runs - 1, 0))
    brow = lax.rem(lax.axis_index("zh") + turn, runs) * lax.axis_size("y") + lax.axis_index("y")
    copies = block_copies(order_ref, feats_ref, out_ref, sems, 0, brow, 1 - zl // 2)
    for copy in copies:
        copy.start()
    for copy in copies:
        copy.wait()


def mask_kernel(counts_ref, grads_ref, out_ref):
    rows = lax.broadcasted_iota(jnp.int32, grads_ref.shape, 0)
    count = counts_ref[lax.axis_index("x") * lax.axis_size("zl") + lax.axis_index("zl")]
    masked = jnp.where(rows < count, grads_ref[...].astype(jnp.float32), 0.0)
    out_ref[...] = masked.astype(jnp.bfloat16)


def grads_copies(grads_ref, out_ref, sems, first):
    half = grads_ref.shape[0] // 2
    width = grads_ref.shape[1]
    return [
        pltpu.make_async_copy(
            grads_ref.at[pl.ds(half * part, half), :],
            out_ref.at[x, pl.ds(first, half), pl.ds(width * part, width)],
            sems.at[x, part],
        )
        for x in range(out_ref.shape[0])
        for part in range(2)
    ]


def own_kernel(order_ref, feats_ref, grads_ref, out_ref, sems, grads_sems):
    half = feats_ref.shape[0] // 2
    brow = lax.axis_index("zh") * lax.axis_size("y") + lax.axis_index("y")
    copies = block_copies(order_ref, feats_ref, out_ref, sems, 0, brow, lax.axis_index("zl") // 2)
    copies += grads_copies(grads_ref, out_ref, grads_sems, 2 * half)
    for copy in copies:
        copy.start()
    for copy in copies:
        copy.wait()


def lent_kernel(feats_ref, grads_ref, filled_ref, out_ref, sems, grads_sems):
    half = feats_ref.shape[1]
    copies = [
        pltpu.make_async_copy(feats_ref.at[x], out_ref.at[x, pl.ds(half, half), :], sems.at[x])
        for x in range(out_ref.shape[0])
    ]
    copies += grads_copies(grads_ref, out_ref, grads_sems, 3 * half)
    for copy in copies:
        copy.start()
    for copy in copies:
        copy.wait()


def lane_sums(value):
    squares = jnp.sum(value * value, axis=0, keepdims=True)
    return squares[:, :128] + squares[:, 128:]


def moment_kernel(
    own_low_ref,
    own_high_ref,
    moment_ref,
    second_ref,
    mine_ref,
    other_ref,
    new_moment_ref,
    new_second_ref,
    sum_ref,
    inner_ref,
    high_ref,
    low_ref,
    left_ref,
):
    quarter = own_low_ref.shape[0]
    half = quarter * 2
    side = lax.axis_index("c")
    part = lax.rem(lax.axis_index("zl"), 2)
    place = lambda i, n: pl.ds(pl.multiple_of(i * n, n), n)
    columns = place(part, half)
    tile = jnp.concatenate([own_low_ref[:, columns], own_high_ref[:, columns]], 0)
    own = jnp.concatenate([own_low_ref[...], own_high_ref[...]], 0)
    new_moment = 0.9 * moment_ref[...] + 0.1 * tile
    new_second = 0.95 * second_ref[...] + 0.05 * tile * tile
    new_moment_ref[...] = new_moment
    new_second_ref[...] = new_second
    sum_ref[...] = lane_sums(new_moment / (jnp.sqrt(new_second) + 1e-08))
    left_ref[place(part, quarter), :] = mine_ref[...]
    left_ref[place(1 - part, quarter), :] = other_ref[...]
    inner_ref[...] = dot_plain(split(left_ref[:, place(side, half)]), split(own))
    high_ref[...], low_ref[...] = split(left_ref[:, place(1 - side, half)])


def step_kernel(
    inner_ref,
    other_low_ref,
    other_high_ref,
    left_high_ref,
    left_low_ref,
    right_mine_ref,
    right_other_ref,
    sum_ref,
    precond_ref,
    sums_ref,
    right_ref,
):
    quarter = right_mine_ref.shape[0]
    side = lax.axis_index("c")
    place = lambda i, n: pl.ds(pl.multiple_of(i * n, n), n)
    right_ref[place(side, quarter), :] = right_mine_ref[...]
    right_ref[place(1 - side, quarter), :] = right_other_ref[...]
    left = (left_high_ref[...], left_low_ref[...])
    other = jnp.concatenate([other_low_ref[...], other_high_ref[...]], 0)
    inner = inner_ref[...] + dot_plain(left, split(other))
    precond = dot_rows(split(inner), split(right_ref[...]))
    precond_ref[...] = precond
    sums = jnp.concatenate([sum_ref[...], lane_sums(precond)], 0)
    sums_ref[...] = jnp.broadcast_to(sums[None], sums_ref.shape)


def scale_kernel(sums_ref, precond_ref, out_ref):
    total = jnp.sum(sums_ref[...], axis=0)
    across = lambda v: jnp.sum(jnp.sum(v, axis=1, keepdims=True), axis=0, keepdims=True)
    scale = jnp.sqrt(across(total[0:1]) / (across(total[1:2]) + 1e-06))
    out_ref[...] = scale * precond_ref[...]


def call(kernel, out_shape, in_specs, out_specs, scratch_shapes=(), aliases=None):
    return pl.pallas_call(
        kernel,
        out_shape=out_shape,
        in_specs=in_specs,
        out_specs=out_specs,
        scratch_shapes=scratch_shapes,
        input_output_aliases=aliases or {},
        compiler_params=pltpu.CompilerParams(vmem_limit_bytes=VMEM_LIMIT),
    )


VM = pl.BlockSpec(memory_space=pltpu.VMEM)
SM = pl.BlockSpec(memory_space=pltpu.SMEM)
ANY = pl.BlockSpec(memory_space=pl.ANY)


def body(
    features,
    out_grads,
    token_counts,
    owner_order,
    moment,
    second,
    left_stat,
    right_stat,
    left_root,
    right_root,
):
    f32 = jnp.float32
    tok_rows = features.shape[0]
    block_size = left_stat.shape[-1]
    half_size = block_size // 2
    quarter = block_size // 4
    side_bit = lax.axis_index("c")
    part_bit = lax.axis_index("zl") % 2
    precise = lax.Precision.HIGH
    token_total = jnp.sum(token_counts).astype(f32)
    left_mine = left_root[0, 0]
    right_mine = right_root[0, 0]

    half_rows = tok_rows // 2
    lines = lax.axis_size("x")
    order = owner_order.T
    lent = call(
        lend_kernel,
        jax.ShapeDtypeStruct((lines, half_rows, block_size), jnp.bfloat16),
        [SM, ANY],
        VM,
        [pltpu.SemaphoreType.DMA((lines,))],
    )(order, features)
    lent = lax.ppermute(lent, ("zl", "zh"), z_partners())
    masked = jax.ShapeDtypeStruct(out_grads.shape, jnp.bfloat16)
    grads = call(mask_kernel, masked, [SM, VM], VM)(token_counts, out_grads)
    lent_grads = lax.ppermute(grads, "zl", [(i, 3 - i) for i in range(4)])
    packed = jax.ShapeDtypeStruct((lines, 4 * half_rows, block_size), jnp.bfloat16)
    sems = [pltpu.SemaphoreType.DMA((lines,)), pltpu.SemaphoreType.DMA((lines, 2))]
    filled = call(own_kernel, packed, [SM, ANY, VM], ANY, sems)(order, features, grads)
    outgoing = call(lent_kernel, packed, [VM, VM, ANY], ANY, sems, {2: 0})(
        lent, lent_grads, filled
    )
    left_other = partner(left_mine, "zl")
    right_other = partner(right_mine, "c")
    arrived = lax.all_to_all(outgoing, "x", split_axis=0, concat_axis=0, tiled=True)
    arrived, left_other, right_other = lax.optimization_barrier(
        (arrived, left_other, right_other)
    )
    feats_own = arrived[:, :tok_rows].reshape(-1, block_size)
    feats_other = partner(feats_own, "c")
    grads_low = arrived[:, tok_rows:, :half_size].reshape(-1, half_size)
    grads_high = arrived[:, tok_rows:, half_size:].reshape(-1, half_size)
    own_first = side_bit == 0
    grads_own = jnp.where(own_first, grads_low, grads_high)
    grads_other = jnp.where(own_first, grads_high, grads_low)
    own_parts, other_parts = [], []
    for at in (slice(0, quarter), slice(quarter, half_size)):
        partial = jnp.dot(
            grads_own[:, at].T, feats_own, preferred_element_type=f32
        ) + jnp.dot(grads_other[:, at].T, feats_other, preferred_element_type=f32)
        own_parts.append((partial + partner(partial, "zl")) / token_total)
        other_parts.append(partner(own_parts[-1], "c"))

    tile = jax.ShapeDtypeStruct((half_size, half_size), f32)
    piece = jax.ShapeDtypeStruct((half_size, half_size), jnp.bfloat16)
    rows = jax.ShapeDtypeStruct((half_size, block_size), f32)
    new_moment, new_second, direction_sum, inner, left_high, left_low = call(
        moment_kernel,
        (tile, tile, jax.ShapeDtypeStruct((1, 128), f32), rows, piece, piece),
        [VM] * 6,
        (VM,) * 6,
        [pltpu.VMEM(rows.shape, f32)],
    )(*own_parts, moment, second, left_mine, left_other)
    near = ("x", "y", "c")
    line = ("zl", "zh")
    precond, sums = call(
        step_kernel,
        (tile, jax.ShapeDtypeStruct((lax.axis_size(near), 2, 128), f32)),
        [VM] * 8,
        (VM,) * 2,
        [pltpu.VMEM(rows.shape, f32)],
    )(inner, *other_parts, left_high, left_low, right_mine, right_other, direction_sum)
    sums = lax.all_to_all(sums, near, split_axis=0, concat_axis=0, tiled=True)
    sums, own_parts, other_parts = lax.optimization_barrier((sums, own_parts, other_parts))
    own_rows = jnp.concatenate(own_parts, 0)
    other_rows = jnp.concatenate(other_parts, 0)
    sums = jnp.broadcast_to(jnp.sum(sums, 0), (lax.axis_size(line), 2, 128))
    sums = lax.all_to_all(sums, line, split_axis=0, concat_axis=0, tiled=True)
    update = call(scale_kernel, tile, [VM, VM], VM)(sums, precond)

    whole_block = jnp.where(
        own_first,
        jnp.concatenate([own_rows, other_rows], 0),
        jnp.concatenate([other_rows, own_rows], 0),
    )
    left_rows = lax.dynamic_slice_in_dim(own_rows, part_bit * quarter, quarter, 0)
    right_cols = lax.dynamic_slice_in_dim(
        whole_block, part_bit * half_size + side_bit * quarter, quarter, 1
    )
    next_left = 0.95 * left_stat[0, 0] + 0.05 * (
        jnp.dot(left_rows, whole_block.T, precision=precise) / block_size
    )
    next_right = 0.95 * right_stat[0, 0] + 0.05 * (
        jnp.dot(right_cols.T, whole_block, precision=precise) / block_size
    )
    return (update, new_moment, new_second, next_left[None, None], next_right[None, None])


def solution(mesh):
    fine = Mesh(mesh.devices.reshape(SIZES), DP + SHARD)
    return jax.shard_map(
        body,
        mesh=fine,
        in_specs=(
            P(DP, None),
            P(DP, SHARD),
            P(),
            P(),
            P(SHARD, DP),
            P(SHARD, DP),
            P(SHARD, DP, None, None),
            P(SHARD, DP, None, None),
            P(SHARD, DP, None, None),
            P(SHARD, DP, None, None),
        ),
        out_specs=(
            P(SHARD, DP),
            P(SHARD, DP),
            P(SHARD, DP),
            P(SHARD, DP, None, None),
            P(SHARD, DP, None, None),
        ),
        check_vma=False,
    )
```
